32 devices in a mesh: groups: 2 (over y), lon: 4 (over z), lat: 2 (over x), sub: 2 (over core).
Axes of the slice: x: 2, y: 2, z: 4, core: 2. Of those that a mesh axis runs over, the one named last changes fastest.
Arguments:
- grid_latent: bfloat16 [32768, 256], P(('groups', 'lon', 'lat', 'sub')), parts along dimension 0, may hold values from -6 to 6
- mesh_latent: float32 [32, 512, 256], P(('groups', 'lat'), ('lon', 'sub')), parts along dimension 0, may hold values from -6 to 6
- block_owner: int32 [128, 1], P(('lon', 'lat', 'sub')), may hold values from 0 to 7; in each aligned block of 8 rows (0 to 7, 8 to 15, ...) at most 2 rows name the same one
- block_sender: int32 [128, 128], P(('lon', 'lat', 'sub')), may hold values from 0 to 1023
- block_receiver: int32 [128, 128], P(('lon', 'lat', 'sub')), may hold values from 0 to 512, as said below
- block_feature: bfloat16 [128, 4, 128], P(('lon', 'lat', 'sub')), may hold values from -6 to 6
- mesh_sender: int32 [256, 128], P(('lon', 'lat', 'sub')), may hold values from 0 to 815, as said below
- mesh_receiver: int32 [256, 128], P(('lon', 'lat', 'sub')), may hold values from 0 to 511
- mesh_feature: bfloat16 [256, 4, 128], P(('lon', 'lat', 'sub')), may hold values from -6 to 6
- encoder_edge_input: bfloat16 [512, 256], replicated, may hold values from -0.25 to 0.25
- encoder_edge_feature: float32 [4, 256], replicated, may hold values from -3 to 3
- encoder_edge_bias: float32 [256], replicated, may hold values from -3 to 3
- encoder_edge_output: bfloat16 [256, 256], replicated, may hold values from -0.375 to 0.375
- encoder_edge_gain: float32 [256], replicated, may hold values from 0.5 to 1.5
- encoder_node_input: bfloat16 [512, 256], replicated, may hold values from -0.25 to 0.25
- encoder_node_bias: float32 [256], replicated, may hold values from -3 to 3
- encoder_node_output: bfloat16 [256, 256], replicated, may hold values from -0.375 to 0.375
- encoder_node_gain: float32 [256], replicated, may hold values from 0.5 to 1.5
- processor_edge_input: bfloat16 [512, 256], replicated, may hold values from -0.25 to 0.25
- processor_edge_feature: float32 [4, 256], replicated, may hold values from -3 to 3
- processor_edge_bias: float32 [256], replicated, may hold values from -3 to 3
- processor_edge_output: bfloat16 [256, 256], replicated, may hold values from -0.375 to 0.375
- processor_edge_gain: float32 [256], replicated, may hold values from 0.5 to 1.5
- processor_node_input: bfloat16 [512, 256], replicated, may hold values from -0.25 to 0.25
- processor_node_bias: float32 [256], replicated, may hold values from -3 to 3
- processor_node_output: bfloat16 [256, 256], replicated, may hold values from -0.375 to 0.375
- processor_node_gain: float32 [256], replicated, may hold values from 0.5 to 1.5
Outputs:
- mesh_out: float32 [32, 512, 256], P(('groups', 'lat'), ('lon', 'sub')), parts along dimension 0
The draws below stay inside these ranges and needn't reach their ends.
There are 2 independent parts, one for each index of `groups`. The reference program is written for one: setup_inputs(seed, part) draws one part's arguments, and reference() takes and returns one part's arrays. A program takes and returns all parts, laid end to end along the dimension named above; an argument that names none is the same for every part. Nothing has to cross between parts.
Inputs may be any that keep to these rules, and one draw needn't show every extreme that they name: `block_owner`: among the 8 blocks of one device no owner is named more than 2 times, a bound that some block reaches. `block_receiver`: each block ends with 1 to 32 padding rows holding 512. `mesh_sender`: A sender cell lies at most 2 rows and 2 columns away from its receiver's cell in the extended block, whose node (a, b) is cell (a + 2) * 68 + b + 2. The first row of each device's first block joins its last node with the last cell, the second row its first node with cell 0.
All inputs are finite; a program needn't handle non-finite values.
Results may differ from the reference program's by a relative error of at most 0.0043.
Values may be sent and summed in bfloat16 or wider, within the bound.
A program may use at most 64 MiB of HBM per device.

```python
import math
import jax
import jax.numpy as jnp
import numpy as np
from jax import lax

LATENT = 256
EDGE_FEAT = 4
EB = 128
CAP = 2
PB_DEV = 16
ML_LAT = 8
ML_LON = 64
W = 2
G_DEV = 1024
M_DEV = 512
PEERS = 8
BLK_DEV = 8
GRID = 16384
BLOCKS = 128
PBLOCKS = 256
NLAT_M = 16
NLON_M = 512
N_LON = 4
N_LAT = 2
N_SUB = 2


def draw_block_receiver(key, part):
    key = jax.random.fold_in(key, 7)
    key_nodes, key_pads = jax.random.split(key)
    receivers = jax.random.randint(key_nodes, (BLOCKS, EB), 0, M_DEV)
    padding = jax.random.randint(key_pads, (BLOCKS, 1), 1, EB // 4 + 1)
    position = jnp.arange(EB)[None, :]
    return jnp.where(position >= EB - padding, M_DEV, receivers).astype(jnp.int32)


def processor_edges(key):
    key_nodes, key_rows, key_cols = jax.random.split(key, 3)
    receivers = jax.random.randint(key_nodes, (PBLOCKS, EB), 0, M_DEV)
    row_step = jax.random.randint(key_rows, (PBLOCKS, EB), -W, W + 1)
    col_step = jax.random.randint(key_cols, (PBLOCKS, EB), -W, W + 1)
    first_block = (jnp.arange(PBLOCKS) % PB_DEV == 0)[:, None]
    position = jnp.arange(EB)[None, :]
    corner_high = first_block & (position == 0)
    corner_low = first_block & (position == 1)
    receivers = jnp.where(corner_high, M_DEV - 1, jnp.where(corner_low, 0, receivers))
    row_step = jnp.where(corner_high, W, jnp.where(corner_low, -W, row_step))
    col_step = jnp.where(corner_high, W, jnp.where(corner_low, -W, col_step))
    senders = (receivers // ML_LON + W + row_step) * (ML_LON + 2 * W) + receivers % ML_LON + W + col_step
    return (senders.astype(jnp.int32), receivers.astype(jnp.int32))


def draw_mesh_sender(key, part):
    return processor_edges(key)[0]


def draw_mesh_receiver(key, part):
    return processor_edges(key)[1]


def set_ends(drawn, rng, least, high):
    place = [jax.random.randint(jax.random.fold_in(rng, axis), (), 0, length) for axis, length in enumerate(drawn.shape)]
    main_axis = drawn.shape.index(max(drawn.shape))
    neighbour = place[:main_axis] + [(place[main_axis] + 1) % drawn.shape[main_axis]] + place[main_axis + 1:]
    return drawn.at[tuple(place)].set(least).at[tuple(neighbour)].set(high)


def shard_levels(key, extent, cuts, least, largest):
    def one(axis_at, blocks):
        steps = jax.random.uniform(jax.random.fold_in(jax.random.fold_in(key, 6), axis_at), (blocks,), jnp.float32, least / len(cuts), largest / len(cuts))
        return jnp.repeat(jnp.exp(steps), extent[axis_at] // blocks).reshape((-1,) + (1,) * (len(extent) - axis_at - 1))

    level = one(*cuts[0])
    for cut in cuts[1:]:
        level = level * one(*cut)
    return level


def shared_out(own_key, own, number, rows, count, top, bound, lean):
    order = jax.random.permutation(own_key, count)
    packed, usual = load_shares(count, rows * top, bound, lean, True), load_shares(count, rows * top, bound, lean, False)
    places = jnp.arange(count)

    def named(tallies, rotation):
        used = int((tallies > 0).sum())
        fixed = max(1, used // 4)
        passed = fixed + (places - fixed + rotation * (used - fixed)) % max(1, count - fixed)
        return jnp.zeros((count,), jnp.int32).at[order[jnp.where(places < fixed, places, passed)]].set(jnp.asarray(tallies, jnp.int32))

    tallies = jnp.where(number % 4 == 0, named(packed, number // 4), named(usual, number - number // 4 - 1))
    mixed = jax.random.permutation(jax.random.fold_in(own, 3), count)
    giver, receiver = mixed[0:count // 2 * 2:2], mixed[1:count // 2 * 2:2]
    margin = jnp.minimum(tallies[giver] - 1, bound - tallies[receiver]) // 2
    margin = jnp.where((giver == order[0]) | (receiver == order[0]) | (tallies[receiver] == 0), 0, jnp.maximum(margin, 0))
    passed = jax.random.randint(jax.random.fold_in(own, 4), (count // 2,), 0, 1 << 20) % (margin + 1)
    tallies = tallies.at[giver].add(-passed).at[receiver].add(passed)
    members = jnp.searchsorted(jnp.cumsum(tallies), jnp.arange(rows * top), side="right").astype(jnp.int32)
    listing = members.reshape(top, rows).T
    listing = listing[jax.random.permutation(jax.random.fold_in(own, 1), rows)]
    rotation = jax.random.randint(jax.random.fold_in(own, 2), (rows, 1), 0, top)
    return jnp.take_along_axis(listing, (jnp.arange(top)[None, :] + rotation) % top, axis=1)


def load_shares(number_of, total, limit, lean, full):
    portions = [(1 << 20) // math.isqrt(rank ** lean) + 1 for rank in range(1, number_of + 1)]
    largest = limit if full else min(limit, max(-(-total // number_of), total * portions[0] // sum(portions)))
    least = 1 if total - largest >= number_of - 1 else 0
    holding, spare = [largest] + [least] * (number_of - 1), total - largest - least * (number_of - 1)
    while spare > 0:
        candidates = [i for i in range(1, number_of) if holding[i] < largest] or [i for i in range(1, number_of) if holding[i] < limit]
        mass, remaining = sum([portions[i] for i in candidates]), spare
        for i in candidates:
            addition = min(limit - holding[i], max(1, remaining * portions[i] // mass), spare)
            holding[i] = holding[i] + addition
            spare = spare - addition
    return np.array(holding)


def noise(rng, extent, scale, bound, cuts=(), kind=jnp.bfloat16):
    level = shard_levels(rng, extent, cuts, -0.22, 0.18) if cuts else 1.0
    array = jax.random.normal(rng, extent, jnp.float32) * scale * level
    return jnp.minimum(jnp.maximum(array, -bound), bound).astype(kind)


def setup_inputs(seed: int = 0, part: int = 0) -> dict:
    splits = jax.random.split(jax.random.key(seed), 28)
    part_splits = jax.random.split(jax.random.fold_in(splits[27], part), 28)
    grid_latent = noise(part_splits[0], (GRID, LATENT), 1.0, 6.0, ((0, 16),))
    mesh_latent = noise(part_splits[1], (NLAT_M, NLON_M, LATENT), 1.0, 6.0, ((0, 2), (1, 8)), jnp.float32)
    block_owner_keys = jax.random.split(jax.random.fold_in(splits[2], 1), BLOCKS // BLK_DEV)
    block_owner_turns = jax.random.permutation(jax.random.fold_in(splits[2], 3), BLOCKS // BLK_DEV)
    block_owner = jax.vmap(lambda own, number: shared_out(jax.random.fold_in(splits[2], 2), own, number, BLK_DEV, PEERS, 1, CAP, 2))(block_owner_keys, block_owner_turns).reshape((BLOCKS, 1))
    block_sender = set_ends(jax.random.randint(splits[3], (BLOCKS, EB), 0, G_DEV), jax.random.fold_in(splits[3], 1), 0, G_DEV - 1).astype(jnp.int32)
    block_receiver = draw_block_receiver(jax.random.fold_in(splits[27], 71), part)
    block_feature = noise(splits[5], (BLOCKS, EDGE_FEAT, EB), 1.0, 6.0, ((0, 16),))
    mesh_sender = draw_mesh_sender(jax.random.fold_in(splits[27], 71), part)
    mesh_receiver = draw_mesh_receiver(jax.random.fold_in(splits[27], 71), part)
    mesh_feature = noise(splits[8], (PBLOCKS, EDGE_FEAT, EB), 1.0, 6.0, ((0, 16),))
    encoder_edge_input = noise(splits[9], (2 * LATENT, LATENT), (2 * LATENT) ** -0.5, 0.25)
    encoder_edge_feature = noise(splits[10], (EDGE_FEAT, LATENT), EDGE_FEAT ** -0.5, 3.0, (), jnp.float32)
    encoder_edge_bias = noise(splits[11], (LATENT,), 0.5, 3.0, (), jnp.float32)
    encoder_edge_output = noise(splits[12], (LATENT, LATENT), LATENT ** -0.5, 0.375)
    encoder_edge_gain = jnp.clip(1.0 + 0.1 * jax.random.normal(splits[13], (LATENT,), jnp.float32), 0.5, 1.5)
    encoder_node_input = noise(splits[14], (2 * LATENT, LATENT), (2 * LATENT) ** -0.5, 0.25)
    encoder_node_bias = noise(splits[15], (LATENT,), 0.5, 3.0, (), jnp.float32)
    encoder_node_output = noise(splits[16], (LATENT, LATENT), LATENT ** -0.5, 0.375)
    encoder_node_gain = jnp.clip(1.0 + 0.1 * jax.random.normal(splits[17], (LATENT,), jnp.float32), 0.5, 1.5)
    processor_edge_input = noise(splits[18], (2 * LATENT, LATENT), (2 * LATENT) ** -0.5, 0.25)
    processor_edge_feature = noise(splits[19], (EDGE_FEAT, LATENT), EDGE_FEAT ** -0.5, 3.0, (), jnp.float32)
    processor_edge_bias = noise(splits[20], (LATENT,), 0.5, 3.0, (), jnp.float32)
    processor_edge_output = noise(splits[21], (LATENT, LATENT), LATENT ** -0.5, 0.375)
    processor_edge_gain = jnp.clip(1.0 + 0.1 * jax.random.normal(splits[22], (LATENT,), jnp.float32), 0.5, 1.5)
    processor_node_input = noise(splits[23], (2 * LATENT, LATENT), (2 * LATENT) ** -0.5, 0.25)
    processor_node_bias = noise(splits[24], (LATENT,), 0.5, 3.0, (), jnp.float32)
    processor_node_output = noise(splits[25], (LATENT, LATENT), LATENT ** -0.5, 0.375)
    processor_node_gain = jnp.clip(1.0 + 0.1 * jax.random.normal(splits[26], (LATENT,), jnp.float32), 0.5, 1.5)
    return {"grid_latent": grid_latent, "mesh_latent": mesh_latent, "block_owner": block_owner, "block_sender": block_sender, "block_receiver": block_receiver, "block_feature": block_feature, "mesh_sender": mesh_sender, "mesh_receiver": mesh_receiver, "mesh_feature": mesh_feature, "encoder_edge_input": encoder_edge_input, "encoder_edge_feature": encoder_edge_feature, "encoder_edge_bias": encoder_edge_bias, "encoder_edge_output": encoder_edge_output, "encoder_edge_gain": encoder_edge_gain, "encoder_node_input": encoder_node_input, "encoder_node_bias": encoder_node_bias, "encoder_node_output": encoder_node_output, "encoder_node_gain": encoder_node_gain, "processor_edge_input": processor_edge_input, "processor_edge_feature": processor_edge_feature, "processor_edge_bias": processor_edge_bias, "processor_edge_output": processor_edge_output, "processor_edge_gain": processor_edge_gain, "processor_node_input": processor_node_input, "processor_node_bias": processor_node_bias, "processor_node_output": processor_node_output, "processor_node_gain": processor_node_gain}


def layer_norm(values, norm_gain):
    center = values - lax.optimization_barrier(jnp.mean(values, axis=-1, keepdims=True))
    spread = lax.optimization_barrier(jnp.mean(center * center, axis=-1, keepdims=True))
    return center * lax.rsqrt(spread + 1e-05) * norm_gain

def edge_update(senders, receivers, features, input_weight, feature_weight, offset, output_weight, norm_gain):
    channels = senders.shape[-1]
    preact = jnp.dot(senders, input_weight[:channels], preferred_element_type=jnp.float32)
    preact = preact + jnp.dot(receivers, input_weight[channels:], preferred_element_type=jnp.float32)
    preact = preact + jnp.dot(features.astype(jnp.float32), feature_weight, precision=lax.Precision.HIGHEST) + offset
    hidden = jax.nn.silu(preact).astype(jnp.bfloat16)
    projected = jnp.dot(hidden, output_weight, preferred_element_type=jnp.float32)
    return layer_norm(projected, norm_gain).astype(jnp.bfloat16)

def node_update(mesh_rows, mesh_bf, summed, input_weight, offset, output_weight, norm_gain):
    channels = mesh_rows.shape[-1]
    preact = jnp.dot(mesh_bf, input_weight[:channels], preferred_element_type=jnp.float32)
    preact = preact + jnp.dot(summed.astype(jnp.bfloat16), input_weight[channels:], preferred_element_type=jnp.float32) + offset
    hidden = jax.nn.silu(preact).astype(jnp.bfloat16)
    projected = jnp.dot(hidden, output_weight, preferred_element_type=jnp.float32)
    return mesh_rows + layer_norm(projected, norm_gain)

def reference(grid_latent, mesh_latent, block_owner, block_sender, block_receiver, block_feature, mesh_sender, mesh_receiver, mesh_feature, encoder_edge_input, encoder_edge_feature, encoder_edge_bias, encoder_edge_output, encoder_edge_gain, encoder_node_input, encoder_node_bias, encoder_node_output, encoder_node_gain, processor_edge_input, processor_edge_feature, processor_edge_bias, processor_edge_output, processor_edge_gain, processor_node_input, processor_node_bias, processor_node_output, processor_node_gain):
    part_count = N_LON * N_LAT * N_SUB
    total_nodes = NLAT_M * NLON_M
    mesh_flat = mesh_latent.reshape(total_nodes, LATENT)
    mesh_bf = mesh_flat.astype(jnp.bfloat16)
    device_ids = jnp.arange(part_count, dtype=jnp.int32)

    def node_global(lat_index, peer_index, local_node):
        row_index = lat_index * ML_LAT + local_node // ML_LON
        col_index = peer_index * ML_LON + local_node % ML_LON
        return row_index * NLON_M + col_index
    owners = block_owner[:, 0].reshape(part_count, BLK_DEV)
    sender_ids = block_sender.reshape(part_count, BLK_DEV * EB)
    receiver_ids = block_receiver.reshape(part_count, BLK_DEV, EB)
    edge_feats = jnp.swapaxes(block_feature, 1, 2).reshape(part_count, BLK_DEV * EB, EDGE_FEAT)

    def encode_device(running, inputs):
        device, owner_peer, senders, receivers, features = inputs
        grid_rows = lax.dynamic_slice_in_dim(grid_latent, (device * G_DEV).astype(jnp.int32), G_DEV, 0)
        send_rows = grid_rows[senders]
        lat_index = device // N_SUB % N_LAT
        target = node_global(lat_index, owner_peer[:, None], receivers)
        target = jnp.where(receivers < M_DEV, target, total_nodes).reshape(-1).astype(jnp.int32)
        recv_rows = mesh_bf[jnp.minimum(target, total_nodes - 1)]
        edge_out = edge_update(send_rows, recv_rows, features, encoder_edge_input, encoder_edge_feature, encoder_edge_bias, encoder_edge_output, encoder_edge_gain)
        return (running.at[target].add(edge_out.astype(jnp.float32), mode='drop'), None)
    start_sum = jnp.zeros((total_nodes, LATENT), jnp.float32)
    enc_sum, _ = lax.scan(encode_device, start_sum, (device_ids, owners, sender_ids, receiver_ids, edge_feats))
    mesh_enc = node_update(mesh_flat, mesh_bf, enc_sum, encoder_node_input, encoder_node_bias, encoder_node_output, encoder_node_gain)
    enc_bf = mesh_enc.astype(jnp.bfloat16)
    padded = jnp.pad(enc_bf.reshape(NLAT_M, NLON_M, LATENT), ((W, W), (0, 0), (0, 0))).reshape(-1, LATENT)
    proc_senders = mesh_sender.reshape(part_count, PB_DEV * EB)
    proc_receivers = mesh_receiver.reshape(part_count, PB_DEV * EB)
    proc_feats = jnp.swapaxes(mesh_feature, 1, 2).reshape(part_count, PB_DEV * EB, EDGE_FEAT)

    def process_device(running, inputs):
        device, senders, receivers, features = inputs
        lat_index = device // N_SUB % N_LAT
        peer_index = device // (N_LAT * N_SUB) * N_SUB + device % N_SUB
        halo_row = senders // (ML_LON + 2 * W)
        halo_col = senders % (ML_LON + 2 * W)
        padded_row = lat_index * ML_LAT + halo_row
        padded_col = (peer_index * ML_LON + halo_col - W) % NLON_M
        send_rows = padded[(padded_row * NLON_M + padded_col).astype(jnp.int32)]
        target = node_global(lat_index, peer_index, receivers).astype(jnp.int32)
        recv_rows = enc_bf[target]
        edge_out = edge_update(send_rows, recv_rows, features, processor_edge_input, processor_edge_feature, processor_edge_bias, processor_edge_output, processor_edge_gain)
        return (running.at[target].add(edge_out.astype(jnp.float32)), None)
    proc_sum, _ = lax.scan(process_device, start_sum, (device_ids, proc_senders, proc_receivers, proc_feats))
    mesh_out = node_update(mesh_enc, enc_bf, proc_sum, processor_node_input, processor_node_bias, processor_node_output, processor_node_gain)
    return mesh_out.reshape(NLAT_M, NLON_M, LATENT)
```

```python
import functools

import jax
import jax.numpy as jnp
from jax import lax
from jax.experimental import pallas as pl
from jax.experimental.pallas import tpu as pltpu
from jax.sharding import PartitionSpec as P

CAP = 2
W = 2
MESH = pl.DeviceIdType.MESH
BF = jnp.bfloat16
F32 = jnp.float32


def dot(a, b):
    return jnp.dot(a, b, preferred_element_type=F32)


def silu(v):
    half = 0.5 * v
    return half + half * jnp.tanh(half)


def layer_norm(values, gain):
    center = values - jnp.mean(values, axis=-1, keepdims=True)
    spread = jnp.mean(center * center, axis=-1, keepdims=True)
    return center * lax.rsqrt(spread + 1e-05) * gain


def one_hot(match):
    return jnp.where(match, 1.0, 0.0).astype(BF)


def split3(w):
    a = w.astype(BF)
    r = w - a.astype(F32)
    b = r.astype(BF)
    c = (r - b.astype(F32)).astype(BF)
    return a, b, c


def feature_term(feat_t, w_ref):
    total = feat_t[:, 0:1] * w_ref[0:1, :]
    for f in range(1, w_ref.shape[0]):
        total = total + feat_t[:, f : f + 1] * w_ref[f : f + 1, :]
    return total


def kernel(
    peers,
    subs,
    lats,
    grid_ref,
    mesh_ref,
    owner_ref,
    bsend_ref,
    brecv_ref,
    bfeat_ref,
    msend_ref,
    mrecv_ref,
    mfeat_ref,
    eei,
    eef,
    eeb,
    eeo,
    eeg,
    eni,
    enb,
    eno,
    eng,
    pei,
    pef,
    peb,
    peo,
    peg,
    pni,
    pnb,
    pno,
    png,
    out_ref,
    gproj,
    blkpre,
    send,
    meta_s,
    recv,
    meta_r,
    acc,
    ptab,
    table,
    packs,
    halo_rows,
    halo_packs,
    menc,
    oh,
    oht,
    fbase,
    send_sem,
    recv_sem,
    msend_sem,
    mrecv_sem,
    hsend_sem,
    hrecv_sem,
):
    grid_rows, ch = grid_ref.shape
    nodes = mesh_ref.shape[0]
    blocks, eb = bsend_ref.shape
    pblocks = msend_ref.shape[0]
    feats = bfeat_ref.shape[1]
    pair = CAP * eb
    lon = lax.axis_index("lon")
    lat = lax.axis_index("lat")
    sub = lax.axis_index("sub")
    me = lon * subs + sub
    half = peers // 2

    def at(p, l=None):
        p = lax.rem(p + 2 * peers, peers)
        place = {"lon": p // subs, "sub": lax.rem(p, subs)}
        if l is not None:
            place["lat"] = l
        return place

    barrier = pltpu.get_barrier_semaphore()

    def greet(k, carry):
        pl.semaphore_signal(barrier, inc=1, device_id=at(me + k), device_id_type=MESH)
        return carry

    lax.fori_loop(1, peers, greet, 0)
    for dl in (-1, 1):

        @pl.when((lat + dl >= 0) & (lat + dl < lats))
        def _():
            for dp in (-1, 0, 1):
                pl.semaphore_signal(
                    barrier, inc=1, device_id=at(me + dp, lat + dl), device_id_type=MESH
                )

    gproj[...] = dot(grid_ref[...], eei[:ch, :]).astype(BF)
    send_t = bsend_ref[...].astype(F32).T.astype(jnp.int32)
    lane_g = lax.broadcasted_iota(jnp.int32, (eb, grid_rows), 1)
    for b in range(blocks):
        picked = dot(one_hot(send_t[:, b : b + 1] == lane_g), gproj[...])
        feat_t = bfeat_ref[b].astype(F32).T
        blkpre[b] = (picked + feature_term(feat_t, eef) + eeb[...]).astype(BF)

    bands = jnp.where(lat > 0, 1, 0) + jnp.where(lat < lats - 1, 1, 0)
    pl.semaphore_wait(barrier, peers - 1 + 3 * bands)

    def offset(i):
        return jnp.where(lax.rem(i, 2) == 0, half + i // 2, half - (i + 1) // 2)

    def fill(k):
        q = lax.rem(me + k, peers)
        n = jnp.int32(0)
        s0 = jnp.int32(0)
        s1 = jnp.int32(0)
        for b in range(blocks):
            m = owner_ref[b, 0] == q
            s0 = jnp.where(m & (n == 0), b, s0)
            s1 = jnp.where(m & (n == 1), b, s1)
            n = n + m.astype(jnp.int32)
        send[k, 0:eb, :] = blkpre[s0]
        send[k, eb:pair, :] = blkpre[s1]
        r0 = brecv_ref[pl.ds(s0, 1), :]
        r1 = brecv_ref[pl.ds(s1, 1), :]
        meta_s[k, 0:1, :] = jnp.where(n > 0, r0, nodes)
        meta_s[k, 1:2, :] = jnp.where(n > 1, r1, nodes)
        meta_s[k, 2:8, :] = jnp.full((6, eb), nodes, jnp.int32)

    def copies(k):
        data = pltpu.make_async_remote_copy(
            src_ref=send.at[k],
            dst_ref=recv.at[k],
            send_sem=send_sem.at[k],
            recv_sem=recv_sem.at[k],
            device_id=at(me + k),
            device_id_type=MESH,
        )
        meta = pltpu.make_async_remote_copy(
            src_ref=meta_s.at[k],
            dst_ref=meta_r.at[k],
            send_sem=msend_sem.at[k],
            recv_sem=mrecv_sem.at[k],
            device_id=at(me + k),
            device_id_type=MESH,
        )
        return data, meta

    def send_step(i, carry):
        k = offset(i)
        fill(k)
        data, meta = copies(k)
        meta.start()
        data.start()
        return carry

    lax.fori_loop(0, peers - 1, send_step, 0)
    fill(0)

    mesh_bf = mesh_ref[...].astype(BF)
    ptab[...] = dot(mesh_bf, eei[ch:, :]).astype(BF)
    acc[...] = jnp.zeros_like(acc)
    cells = 68
    rows = nodes // 64
    s = msend_ref[...]
    a = lax.shift_right_logical(s * 241, 14)
    b_ = s - a * cells - W
    a = a - W
    above = a < 0
    below = a >= rows
    row_id = jnp.where(above, a + rows + W, jnp.where(below, a + W, a))
    local = jnp.where(above, a + rows, jnp.where(below, a - rows, a))
    which = jnp.where(above, 0, jnp.where(below, 2, 1))
    base = nodes + 2 * W * 64
    left = b_ < 0
    inner = (~left) & (b_ < 64)
    side = jnp.where(left, 0, 3)
    bb = jnp.where(left, b_ + W, b_ - 64)
    cell = jnp.where(inner, row_id * 64 + b_, base + (side + which) * 16 + local * W + bb)
    cell_t = cell.astype(F32).T.astype(jnp.int32)
    mrecv = mrecv_ref[...]
    recv_base = base + 96
    mrecv_t = (mrecv + recv_base).astype(F32).T.astype(jnp.int32)
    width = table.shape[0]
    lane_t = lax.broadcasted_iota(jnp.int32, (eb, width), 1)
    sub_n = lax.broadcasted_iota(jnp.int32, (nodes, eb), 0)
    for b in range(pblocks):
        hit = (cell_t[:, b : b + 1] == lane_t) | (mrecv_t[:, b : b + 1] == lane_t)
        oh[pl.ds(b * eb, eb), :] = one_hot(hit)
        oht[:, pl.ds(b * eb, eb)] = one_hot(sub_n == mrecv[b : b + 1, :])
        feat_t = mfeat_ref[b].astype(F32).T
        fbase[pl.ds(b * eb, eb), :] = feature_term(feat_t, pef) + peb[...]

    lane_n = lax.broadcasted_iota(jnp.int32, (eb, nodes), 1)

    def encode(data, meta):
        ids = meta[...]
        ids_t = ids.astype(F32).T.astype(jnp.int32)
        parts = []
        for j in range(CAP):
            picked = dot(one_hot(ids_t[:, j : j + 1] == lane_n), ptab[...])
            pre = picked + data[pl.ds(j * eb, eb), :].astype(F32)
            parts.append(silu(pre).astype(BF))
        hidden = jnp.concatenate(parts, axis=0)
        edges = layer_norm(dot(hidden, eeo[...]), eeg[...]).astype(BF)
        spread = jnp.concatenate(
            [one_hot(sub_n == ids[j : j + 1, :]) for j in range(CAP)], axis=1
        )
        acc[...] += dot(spread, edges)

    encode(send.at[0], meta_s.at[0])

    def recv_step(i, carry):
        k = offset(i)
        data, meta = copies(k)
        meta.wait()
        data.wait()
        encode(recv.at[k], meta_r.at[k])
        return carry

    lax.fori_loop(0, peers - 1, recv_step, 0)

    def node(own_bf, summed, w_in, bias, w_out, gain):
        pre = dot(own_bf, w_in[:ch, :]) + dot(summed.astype(BF), w_in[ch:, :]) + bias[...]
        return layer_norm(dot(silu(pre).astype(BF), w_out[...]), gain[...])

    mesh_enc = mesh_ref[...] + node(mesh_bf, acc[...], eni, enb, eno, eng)
    menc[...] = mesh_enc
    enc_bf = mesh_enc.astype(BF)
    own = dot(enc_bf, pei[:ch, :]).astype(BF)
    table[0:nodes, :] = own
    pick_r = lax.broadcasted_iota(jnp.int32, (32, nodes), 0)
    pick_n = lax.broadcasted_iota(jnp.int32, (32, nodes), 1)
    r16 = pick_r & 15
    wanted = (r16 >> 1) * 64 + (r16 & 1) + jnp.where(pick_r < 16, 62, 0)
    packed = dot(one_hot(wanted == pick_n), own).astype(BF)
    packs[0] = packed[0:16]
    packs[1] = packed[16:32]

    edge = W * 64

    def side_copy(dp, dl):
        n = (0 if dp == 1 else 3) + (1 - dl)
        return pltpu.make_async_remote_copy(
            src_ref=packs.at[0 if dp == 1 else 1],
            dst_ref=halo_packs.at[n],
            send_sem=hsend_sem.at[n],
            recv_sem=hrecv_sem.at[n],
            device_id=at(me + dp, lat + dl),
            device_id_type=MESH,
        )

    def band_copy(dl):
        n = 0 if dl == 1 else 1
        first = nodes - edge if dl == 1 else 0
        return pltpu.make_async_remote_copy(
            src_ref=table.at[pl.ds(first, edge), :],
            dst_ref=halo_rows.at[n],
            send_sem=hsend_sem.at[6 + n],
            recv_sem=hrecv_sem.at[6 + n],
            device_id=at(me, lat + dl),
            device_id_type=MESH,
        )

    def inside(dl):
        return (lat + dl >= 0) & (lat + dl < lats)

    for dl in (-1, 1):

        @pl.when(inside(dl))
        def _():
            band_copy(dl).start()
            side_copy(1, dl).start()
            side_copy(-1, dl).start()

    side_copy(1, 0).start()
    side_copy(-1, 0).start()
    table[recv_base : recv_base + nodes, :] = dot(enc_bf, pei[ch:, :]).astype(BF)
    table[recv_base + nodes :, :] = jnp.zeros((width - recv_base - nodes, ch), BF)
    own_in = dot(enc_bf, pni[:ch, :]) + pnb[...]

    for dl in (-1, 1):
        n = 0 if dl == -1 else 1
        slots = (0, 3) if dl == -1 else (2, 5)

        @pl.when(inside(dl))
        def _():
            band_copy(-dl).wait_recv()
            side_copy(1, -dl).wait_recv()
            side_copy(-1, -dl).wait_recv()
            table[pl.ds(nodes + n * edge, edge), :] = halo_rows[n]
            for m in slots:
                table[pl.ds(base + m * 16, 16), :] = halo_packs[m]

        @pl.when(jnp.logical_not(inside(dl)))
        def _():
            table[pl.ds(nodes + n * edge, edge), :] = jnp.zeros((edge, ch), BF)
            for m in slots:
                table[pl.ds(base + m * 16, 16), :] = jnp.zeros((16, ch), BF)

    side_copy(1, 0).wait_recv()
    side_copy(-1, 0).wait_recv()
    table[pl.ds(base + 16, 16), :] = halo_packs[1]
    table[pl.ds(base + 64, 16), :] = halo_packs[4]

    acc[...] = jnp.zeros_like(acc)
    step = 4 * eb

    def process(i, carry):
        first = pl.multiple_of(i * step, step)
        pre = dot(oh[pl.ds(first, step), :], table[...]) + fbase[pl.ds(first, step), :]
        hidden = silu(pre).astype(BF)
        edges = layer_norm(dot(hidden, peo[...]), peg[...]).astype(BF)
        acc[...] += dot(oht[:, pl.ds(first, step)], edges)
        return carry

    lax.fori_loop(0, pblocks * eb // step, process, 0)
    pre = own_in + dot(acc[...].astype(BF), pni[ch:, :])
    out_ref[...] = menc[...] + layer_norm(dot(silu(pre).astype(BF), pno[...]), png[...])

    for dl in (-1, 1):

        @pl.when(inside(dl))
        def _():
            band_copy(dl).wait_send()
            side_copy(1, dl).wait_send()
            side_copy(-1, dl).wait_send()

    side_copy(1, 0).wait_send()
    side_copy(-1, 0).wait_send()


def on_device(
    grid_latent,
    mesh_latent,
    block_owner,
    block_sender,
    block_receiver,
    block_feature,
    mesh_sender,
    mesh_receiver,
    mesh_feature,
    *weights,
):
    subs = lax.axis_size("sub")
    peers = lax.axis_size("lon") * subs
    lats = lax.axis_size("lat")
    rows_lat, rows_lon, ch = mesh_latent.shape
    nodes = rows_lat * rows_lon
    blocks, eb = block_sender.shape
    pblocks = mesh_sender.shape[0]
    weights = [w.reshape(1, -1) if w.ndim == 1 else w for w in weights]
    width = 1408
    vm = pl.BlockSpec(memory_space=pltpu.VMEM)
    sm = pl.BlockSpec(memory_space=pltpu.SMEM)
    dma = pltpu.SemaphoreType.DMA
    out = pl.pallas_call(
        functools.partial(kernel, peers, subs, lats),
        out_shape=jax.ShapeDtypeStruct((nodes, ch), F32),
        in_specs=[vm, vm, sm] + [vm] * (6 + len(weights)),
        out_specs=vm,
        scratch_shapes=[
            pltpu.VMEM(grid_latent.shape, BF),
            pltpu.VMEM((blocks, eb, ch), BF),
            pltpu.VMEM((peers, CAP * eb, ch), BF),
            pltpu.VMEM((peers, 8, eb), jnp.int32),
            pltpu.VMEM((peers, CAP * eb, ch), BF),
            pltpu.VMEM((peers, 8, eb), jnp.int32),
            pltpu.VMEM((nodes, ch), F32),
            pltpu.VMEM((nodes, ch), BF),
            pltpu.VMEM((width, ch), BF),
            pltpu.VMEM((2, 16, ch), BF),
            pltpu.VMEM((2, W * rows_lon, ch), BF),
            pltpu.VMEM((6, 16, ch), BF),
            pltpu.VMEM((nodes, ch), F32),
            pltpu.VMEM((pblocks * eb, width), BF),
            pltpu.VMEM((nodes, pblocks * eb), BF),
            pltpu.VMEM((pblocks * eb, ch), F32),
            dma((peers,)),
            dma((peers,)),
            dma((peers,)),
            dma((peers,)),
            dma((8,)),
            dma((8,)),
        ],
        compiler_params=pltpu.CompilerParams(
            collective_id=0, has_side_effects=True, vmem_limit_bytes=50 * 1024 * 1024
        ),
    )(
        grid_latent,
        mesh_latent.reshape(nodes, ch),
        block_owner,
        block_sender,
        block_receiver,
        block_feature,
        mesh_sender,
        mesh_receiver,
        mesh_feature,
        *weights,
    )
    return out.reshape(rows_lat, rows_lon, ch)


def solution(mesh):
    band = P(("lon", "lat", "sub"), None)
    band3 = P(("lon", "lat", "sub"), None, None)
    place = P(("groups", "lat"), ("lon", "sub"), None)
    in_specs = (
        P(("groups", "lon", "lat", "sub"), None),
        place,
        band,
        band,
        band,
        band3,
        band,
        band,
        band3,
    ) + (P(),) * 18
    return jax.shard_map(
        on_device, mesh=mesh, in_specs=in_specs, out_specs=place, check_vma=False
    )
```

```python
import functools

import jax
import jax.numpy as jnp
from jax import lax
from jax.experimental import pallas as pl
from jax.experimental.pallas import tpu as pltpu
from jax.sharding import PartitionSpec as P

CAP = 2
W = 2
MESH = pl.DeviceIdType.MESH
BF = jnp.bfloat16
F32 = jnp.float32


def dot(a, b):
    return jnp.dot(a, b, preferred_element_type=F32)


def silu(v):
    half = 0.5 * v
    return half + half * jnp.tanh(half)


def layer_norm(values, gain):
    center = values - jnp.mean(values, axis=-1, keepdims=True)
    spread = jnp.mean(center * center, axis=-1, keepdims=True)
    return center * lax.rsqrt(spread + 1e-05) * gain


def one_hot(match):
    return jnp.where(match, 1.0, 0.0).astype(BF)


def feature_term(feat_t, w_ref):
    total = feat_t[:, 0:1] * w_ref[0:1, :]
    for f in range(1, w_ref.shape[0]):
        total = total + feat_t[:, f : f + 1] * w_ref[f : f + 1, :]
    return total


def kernel(
    peers,
    subs,
    lats,
    *refs,
):
    inputs, rest = refs[:27], refs[27:]
    (
        out_ref,
        gproj,
        blkpre,
        send,
        meta_s,
        recv,
        meta_r,
        acc,
        ptab,
        table,
        packs,
        halo_rows,
        halo_packs,
        menc,
        oh,
        oht,
        fbase,
        pedges,
        send_sem,
        recv_sem,
        msend_sem,
        mrecv_sem,
        hsend_sem,
        hrecv_sem,
        in_sem,
    ) = rest[:25]
    staged = rest[25:]
    loads = [
        pltpu.make_async_copy(src, dst, in_sem.at[n])
        for n, (src, dst) in enumerate(zip(inputs, staged))
    ]
    early = [3, 0, 9, 5, 10, 11, 2, 4]
    late = [n for n in range(27) if n not in early]
    for n in early + late:
        loads[n].start()
    (
        grid_ref,
        mesh_ref,
        owner_ref,
        bsend_ref,
        brecv_ref,
        bfeat_ref,
        msend_ref,
        mrecv_ref,
        mfeat_ref,
        eei,
        eef,
        eeb,
        eeo,
        eeg,
        eni,
        enb,
        eno,
        eng,
        pei,
        pef,
        peb,
        peo,
        peg,
        pni,
        pnb,
        pno,
        png,
    ) = staged
    grid_rows, ch = grid_ref.shape
    nodes = mesh_ref.shape[0]
    blocks, eb = bsend_ref.shape
    pblocks = msend_ref.shape[0]
    feats = bfeat_ref.shape[1]
    pair = CAP * eb
    lon = lax.axis_index("lon")
    lat = lax.axis_index("lat")
    sub = lax.axis_index("sub")
    me = lon * subs + sub
    half = peers // 2

    def at(p, l=None):
        p = lax.rem(p + 2 * peers, peers)
        place = {"lon": p // subs, "sub": lax.rem(p, subs)}
        if l is not None:
            place["lat"] = l
        return place

    barrier = pltpu.get_barrier_semaphore()

    def greet(k, carry):
        pl.semaphore_signal(barrier, inc=1, device_id=at(me + k), device_id_type=MESH)
        return carry

    lax.fori_loop(1, peers, greet, 0)
    for dl in (-1, 1):

        @pl.when((lat + dl >= 0) & (lat + dl < lats))
        def _():
            for dp in (-1, 0, 1):
                pl.semaphore_signal(
                    barrier, inc=1, device_id=at(me + dp, lat + dl), device_id_type=MESH
                )

    for n in early:
        loads[n].wait()
    gproj[...] = dot(grid_ref[...], eei[:ch, :]).astype(BF)
    send_t = bsend_ref[...].astype(F32).T.astype(jnp.int32)
    lane_g = lax.broadcasted_iota(jnp.int32, (eb, grid_rows), 1)
    for b in range(blocks):
        picked = dot(one_hot(send_t[:, b : b + 1] == lane_g), gproj[...])
        feat_t = bfeat_ref[b].astype(F32).T
        blkpre[b] = (picked + feature_term(feat_t, eef) + eeb[...]).astype(BF)

    bands = jnp.where(lat > 0, 1, 0) + jnp.where(lat < lats - 1, 1, 0)
    pl.semaphore_wait(barrier, peers - 1 + 3 * bands)

    def offset(i):
        return jnp.where(lax.rem(i, 2) == 0, half + i // 2, half - (i + 1) // 2)

    def fill(k):
        q = lax.rem(me + k, peers)
        n = jnp.int32(0)
        s0 = jnp.int32(0)
        s1 = jnp.int32(0)
        for b in range(blocks):
            m = owner_ref[0, b] == q
            s0 = jnp.where(m & (n == 0), b, s0)
            s1 = jnp.where(m & (n == 1), b, s1)
            n = n + m.astype(jnp.int32)
        send[k, 0:eb, :] = blkpre[s0]
        send[k, eb:pair, :] = blkpre[s1]
        r0 = brecv_ref[pl.ds(s0, 1), :]
        r1 = brecv_ref[pl.ds(s1, 1), :]
        meta_s[k, 0:1, :] = jnp.where(n > 0, r0, nodes)
        meta_s[k, 1:2, :] = jnp.where(n > 1, r1, nodes)
        meta_s[k, 2:8, :] = jnp.full((6, eb), nodes, jnp.int32)

    def copies(k):
        data = pltpu.make_async_remote_copy(
            src_ref=send.at[k],
            dst_ref=recv.at[k],
            send_sem=send_sem.at[k],
            recv_sem=recv_sem.at[k],
            device_id=at(me + k),
            device_id_type=MESH,
        )
        meta = pltpu.make_async_remote_copy(
            src_ref=meta_s.at[k],
            dst_ref=meta_r.at[k],
            send_sem=msend_sem.at[k],
            recv_sem=mrecv_sem.at[k],
            device_id=at(me + k),
            device_id_type=MESH,
        )
        return data, meta

    def send_step(i, carry):
        k = offset(i)
        fill(k)
        data, meta = copies(k)
        meta.start()
        data.start()
        return carry

    lax.fori_loop(0, peers - 1, send_step, 0)
    fill(0)

    for n in late:
        loads[n].wait()
    mesh_bf = mesh_ref[...].astype(BF)
    ptab[...] = dot(mesh_bf, eei[ch:, :]).astype(BF)
    acc[...] = jnp.zeros_like(acc)
    cells = 68
    rows = nodes // 64
    s = msend_ref[...]
    a = lax.shift_right_logical(s * 241, 14)
    b_ = s - a * cells - W
    a = a - W
    above = a < 0
    below = a >= rows
    row_id = jnp.where(above, a + rows + W, jnp.where(below, a + W, a))
    local = jnp.where(above, a + rows, jnp.where(below, a - rows, a))
    which = jnp.where(above, 0, jnp.where(below, 2, 1))
    edge = W * 64
    halo = 2 * nodes
    base = halo + 2 * edge
    left = b_ < 0
    inner = (~left) & (b_ < 64)
    side = jnp.where(left, 0, 3)
    bb = jnp.where(left, b_ + W, b_ - 64)
    inside_id = row_id * 64 + b_ + jnp.where(row_id < rows, 0, nodes)
    cell = jnp.where(inner, inside_id, base + (side + which) * 16 + local * W + bb)
    cell_t = cell.astype(F32).T.astype(jnp.int32)
    mrecv = mrecv_ref[...]
    recv_base = nodes
    mrecv_t = (mrecv + recv_base).astype(F32).T.astype(jnp.int32)
    width = table.shape[0]
    lane_t = lax.broadcasted_iota(jnp.int32, (eb, width), 1)
    sub_n = lax.broadcasted_iota(jnp.int32, (nodes, eb), 0)
    for b in range(pblocks):
        hit = (cell_t[:, b : b + 1] == lane_t) | (mrecv_t[:, b : b + 1] == lane_t)
        oh[pl.ds(b * eb, eb), :] = one_hot(hit)
        oht[:, pl.ds(b * eb, eb)] = one_hot(sub_n == mrecv[b : b + 1, :])
        feat_t = mfeat_ref[b].astype(F32).T
        fbase[pl.ds(b * eb, eb), :] = feature_term(feat_t, pef) + peb[...]

    lane_n = lax.broadcasted_iota(jnp.int32, (eb, nodes), 1)

    def encode(data, meta):
        ids = meta[...]
        ids_t = ids.astype(F32).T.astype(jnp.int32)
        parts = []
        for j in range(CAP):
            picked = dot(one_hot(ids_t[:, j : j + 1] == lane_n), ptab[...])
            pre = picked + data[pl.ds(j * eb, eb), :].astype(F32)
            parts.append(silu(pre).astype(BF))
        hidden = jnp.concatenate(parts, axis=0)
        edges = layer_norm(dot(hidden, eeo[...]), eeg[...]).astype(BF)
        spread = jnp.concatenate(
            [one_hot(sub_n == ids[j : j + 1, :]) for j in range(CAP)], axis=1
        )
        acc[...] += dot(spread, edges)

    encode(send.at[0], meta_s.at[0])

    def recv_step(i, carry):
        k = offset(i)
        data, meta = copies(k)
        meta.wait()
        data.wait()
        encode(recv.at[k], meta_r.at[k])
        return carry

    lax.fori_loop(0, peers - 1, recv_step, 0)

    def node(own_bf, summed, w_in, bias, w_out, gain):
        pre = dot(own_bf, w_in[:ch, :]) + dot(summed.astype(BF), w_in[ch:, :]) + bias[...]
        return layer_norm(dot(silu(pre).astype(BF), w_out[...]), gain[...])

    mesh_enc = mesh_ref[...] + node(mesh_bf, acc[...], eni, enb, eno, eng)
    menc[...] = mesh_enc
    enc_bf = mesh_enc.astype(BF)
    own = dot(enc_bf, pei[:ch, :]).astype(BF)
    table[0:nodes, :] = own
    pick_r = lax.broadcasted_iota(jnp.int32, (32, nodes), 0)
    pick_n = lax.broadcasted_iota(jnp.int32, (32, nodes), 1)
    r16 = pick_r & 15
    wanted = (r16 >> 1) * 64 + (r16 & 1) + jnp.where(pick_r < 16, 62, 0)
    packed = dot(one_hot(wanted == pick_n), own).astype(BF)
    packs[0] = packed[0:16]
    packs[1] = packed[16:32]

    def side_copy(dp, dl):
        n = (0 if dp == 1 else 3) + (1 - dl)
        return pltpu.make_async_remote_copy(
            src_ref=packs.at[0 if dp == 1 else 1],
            dst_ref=halo_packs.at[n],
            send_sem=hsend_sem.at[n],
            recv_sem=hrecv_sem.at[n],
            device_id=at(me + dp, lat + dl),
            device_id_type=MESH,
        )

    def band_copy(dl):
        n = 0 if dl == 1 else 1
        first = nodes - edge if dl == 1 else 0
        return pltpu.make_async_remote_copy(
            src_ref=table.at[pl.ds(first, edge), :],
            dst_ref=halo_rows.at[n],
            send_sem=hsend_sem.at[6 + n],
            recv_sem=hrecv_sem.at[6 + n],
            device_id=at(me, lat + dl),
            device_id_type=MESH,
        )

    def inside(dl):
        return (lat + dl >= 0) & (lat + dl < lats)

    for dl in (-1, 1):

        @pl.when(inside(dl))
        def _():
            band_copy(dl).start()
            side_copy(1, dl).start()
            side_copy(-1, dl).start()

    side_copy(1, 0).start()
    side_copy(-1, 0).start()
    table[recv_base : recv_base + nodes, :] = dot(enc_bf, pei[ch:, :]).astype(BF)
    table[base + 96 :, :] = jnp.zeros((width - base - 96, ch), BF)
    step = 4 * eb
    chunks = pblocks * eb // step
    for i in range(chunks):
        part = pl.ds(i * step, step)
        fbase[part, :] += dot(oh[part, :halo], table[:halo, :])
    own_in = dot(enc_bf, pni[:ch, :]) + pnb[...]

    for dl in (-1, 1):
        n = 0 if dl == -1 else 1
        slots = (0, 3) if dl == -1 else (2, 5)

        @pl.when(inside(dl))
        def _():
            band_copy(-dl).wait_recv()
            side_copy(1, -dl).wait_recv()
            side_copy(-1, -dl).wait_recv()
            table[pl.ds(halo + n * edge, edge), :] = halo_rows[n]
            for m in slots:
                table[pl.ds(base + m * 16, 16), :] = halo_packs[m]

        @pl.when(jnp.logical_not(inside(dl)))
        def _():
            table[pl.ds(halo + n * edge, edge), :] = jnp.zeros((edge, ch), BF)
            for m in slots:
                table[pl.ds(base + m * 16, 16), :] = jnp.zeros((16, ch), BF)

    side_copy(1, 0).wait_recv()
    side_copy(-1, 0).wait_recv()
    table[pl.ds(base + 16, 16), :] = halo_packs[1]
    table[pl.ds(base + 64, 16), :] = halo_packs[4]

    for i in range(chunks):
        part = pl.ds(i * step, step)
        pre = fbase[part, :] + dot(oh[part, halo:], table[halo:, :])
        projected = dot(silu(pre).astype(BF), peo[...])
        pedges[part, :] = layer_norm(projected, peg[...]).astype(BF)
    summed = dot(oht[...], pedges[...])
    pre = own_in + dot(summed.astype(BF), pni[ch:, :])
    out_ref[...] = menc[...] + layer_norm(dot(silu(pre).astype(BF), pno[...]), png[...])

    for dl in (-1, 1):

        @pl.when(inside(dl))
        def _():
            band_copy(dl).wait_send()
            side_copy(1, dl).wait_send()
            side_copy(-1, dl).wait_send()

    side_copy(1, 0).wait_send()
    side_copy(-1, 0).wait_send()


def on_device(
    grid_latent,
    mesh_latent,
    block_owner,
    block_sender,
    block_receiver,
    block_feature,
    mesh_sender,
    mesh_receiver,
    mesh_feature,
    *weights,
):
    subs = lax.axis_size("sub")
    peers = lax.axis_size("lon") * subs
    lats = lax.axis_size("lat")
    rows_lat, rows_lon, ch = mesh_latent.shape
    nodes = rows_lat * rows_lon
    blocks, eb = block_sender.shape
    pblocks = mesh_sender.shape[0]
    weights = [w.reshape(1, -1) if w.ndim == 1 else w for w in weights]
    width = 1408
    inputs = [
        grid_latent,
        mesh_latent.reshape(nodes, ch),
        block_owner.reshape(1, blocks),
        block_sender,
        block_receiver,
        block_feature,
        mesh_sender,
        mesh_receiver,
        mesh_feature,
        *weights,
    ]
    staged = [
        (pltpu.SMEM if n == 2 else pltpu.VMEM)(x.shape, x.dtype) for n, x in enumerate(inputs)
    ]
    dma = pltpu.SemaphoreType.DMA
    out = pl.pallas_call(
        functools.partial(kernel, peers, subs, lats),
        out_shape=jax.ShapeDtypeStruct((nodes, ch), F32),
        in_specs=[pl.BlockSpec(memory_space=pl.ANY)] * len(inputs),
        out_specs=pl.BlockSpec(memory_space=pltpu.VMEM),
        scratch_shapes=[
            pltpu.VMEM(grid_latent.shape, BF),
            pltpu.VMEM((blocks, eb, ch), BF),
            pltpu.VMEM((peers, CAP * eb, ch), BF),
            pltpu.VMEM((peers, 8, eb), jnp.int32),
            pltpu.VMEM((peers, CAP * eb, ch), BF),
            pltpu.VMEM((peers, 8, eb), jnp.int32),
            pltpu.VMEM((nodes, ch), F32),
            pltpu.VMEM((nodes, ch), BF),
            pltpu.VMEM((width, ch), BF),
            pltpu.VMEM((2, 16, ch), BF),
            pltpu.VMEM((2, W * rows_lon, ch), BF),
            pltpu.VMEM((6, 16, ch), BF),
            pltpu.VMEM((nodes, ch), F32),
            pltpu.VMEM((pblocks * eb, width), BF),
            pltpu.VMEM((nodes, pblocks * eb), BF),
            pltpu.VMEM((pblocks * eb, ch), F32),
            pltpu.VMEM((pblocks * eb, ch), BF),
            dma((peers,)),
            dma((peers,)),
            dma((peers,)),
            dma((peers,)),
            dma((8,)),
            dma((8,)),
            dma((len(inputs),)),
        ]
        + staged,
        compiler_params=pltpu.CompilerParams(
            collective_id=0, has_side_effects=True, vmem_limit_bytes=64 * 1024 * 1024
        ),
    )(*inputs)
    return out.reshape(rows_lat, rows_lon, ch)


def solution(mesh):
    band = P(("lon", "lat", "sub"), None)
    band3 = P(("lon", "lat", "sub"), None, None)
    place = P(("groups", "lat"), ("lon", "sub"), None)
    in_specs = (
        P(("groups", "lon", "lat", "sub"), None),
        place,
        band,
        band,
        band,
        band3,
        band,
        band,
        band3,
    ) + (P(),) * 18
    return jax.shard_map(
        on_device, mesh=mesh, in_specs=in_specs, out_specs=place, check_vma=False
    )
```

```python
import functools

import jax
import jax.numpy as jnp
from jax import lax
from jax.experimental import pallas as pl
from jax.experimental.pallas import tpu as pltpu
from jax.sharding import PartitionSpec as P

CAP = 2
W = 2
MESH = pl.DeviceIdType.MESH
BF = jnp.bfloat16
F32 = jnp.float32


def dot(a, b):
    return jnp.dot(a, b, preferred_element_type=F32)


def silu(v):
    half = 0.5 * v
    return half + half * jnp.tanh(half)


def layer_norm(values, gain):
    center = values - jnp.mean(values, axis=-1, keepdims=True)
    spread = jnp.mean(center * center, axis=-1, keepdims=True)
    return center * lax.rsqrt(spread + 1e-05) * gain


def one_hot(match):
    return jnp.where(match, 1.0, 0.0).astype(BF)


def feature_term(feat_t, w_ref):
    total = feat_t[:, 0:1] * w_ref[0:1, :]
    for f in range(1, w_ref.shape[0]):
        total = total + feat_t[:, f : f + 1] * w_ref[f : f + 1, :]
    return total


def kernel(
    peers,
    subs,
    lats,
    *refs,
):
    inputs, rest = refs[:27], refs[27:]
    (
        out_ref,
        gproj,
        blkpre,
        send,
        meta_s,
        recv,
        meta_r,
        acc,
        ptab,
        table,
        packs,
        halo_rows,
        halo_packs,
        menc,
        oh,
        oht,
        fbase,
        pedges,
        picks,
        spread,
        send_sem,
        recv_sem,
        msend_sem,
        mrecv_sem,
        hsend_sem,
        hrecv_sem,
        in_sem,
    ) = rest[:27]
    staged = rest[27:]
    loads = [
        pltpu.make_async_copy(src, dst, in_sem.at[n])
        for n, (src, dst) in enumerate(zip(inputs, staged))
    ]
    early = [3, 0, 9, 5, 10, 11, 2, 4]
    late = [n for n in range(27) if n not in early]
    for n in early + late:
        loads[n].start()
    (
        grid_ref,
        mesh_ref,
        owner_ref,
        bsend_ref,
        brecv_ref,
        bfeat_ref,
        msend_ref,
        mrecv_ref,
        mfeat_ref,
        eei,
        eef,
        eeb,
        eeo,
        eeg,
        eni,
        enb,
        eno,
        eng,
        pei,
        pef,
        peb,
        peo,
        peg,
        pni,
        pnb,
        pno,
        png,
    ) = staged
    grid_rows, ch = grid_ref.shape
    nodes = mesh_ref.shape[0]
    blocks, eb = bsend_ref.shape
    pblocks = msend_ref.shape[0]
    feats = bfeat_ref.shape[1]
    pair = CAP * eb
    lon = lax.axis_index("lon")
    lat = lax.axis_index("lat")
    sub = lax.axis_index("sub")
    me = lon * subs + sub

    def at(p, l=None):
        p = lax.rem(p + 2 * peers, peers)
        place = {"lon": p // subs, "sub": lax.rem(p, subs)}
        if l is not None:
            place["lat"] = l
        return place

    barrier = pltpu.get_barrier_semaphore()

    def greet(k, carry):
        pl.semaphore_signal(barrier, inc=1, device_id=at(me + k), device_id_type=MESH)
        return carry

    lax.fori_loop(1, peers, greet, 0)
    for dl in (-1, 1):

        @pl.when((lat + dl >= 0) & (lat + dl < lats))
        def _():
            for dp in (-1, 0, 1):
                pl.semaphore_signal(
                    barrier, inc=1, device_id=at(me + dp, lat + dl), device_id_type=MESH
                )

    for n in early:
        loads[n].wait()
    gproj[...] = dot(grid_ref[...], eei[:ch, :]).astype(BF)
    send_t = bsend_ref[...].astype(F32).T.astype(jnp.int32)
    lane_g = lax.broadcasted_iota(jnp.int32, (eb, grid_rows), 1)
    for b in range(blocks):
        picked = dot(one_hot(send_t[:, b : b + 1] == lane_g), gproj[...])
        feat_t = bfeat_ref[b].astype(F32).T
        blkpre[b] = (picked + feature_term(feat_t, eef) + eeb[...]).astype(BF)

    bands = jnp.where(lat > 0, 1, 0) + jnp.where(lat < lats - 1, 1, 0)
    pl.semaphore_wait(barrier, peers - 1 + 3 * bands)

    def offset(i):
        return jnp.where(lax.rem(i, 2) == 0, 1 + i // 2, peers - 1 - i // 2)

    def fill(k):
        q = lax.rem(me + k, peers)
        n = jnp.int32(0)
        s0 = jnp.int32(0)
        s1 = jnp.int32(0)
        for b in range(blocks):
            m = owner_ref[0, b] == q
            s0 = jnp.where(m & (n == 0), b, s0)
            s1 = jnp.where(m & (n == 1), b, s1)
            n = n + m.astype(jnp.int32)
        send[k, 0:eb, :] = blkpre[s0]
        send[k, eb:pair, :] = blkpre[s1]
        r0 = brecv_ref[pl.ds(s0, 1), :]
        r1 = brecv_ref[pl.ds(s1, 1), :]
        meta_s[k, 0:1, :] = jnp.where(n > 0, r0, nodes)
        meta_s[k, 1:2, :] = jnp.where(n > 1, r1, nodes)
        meta_s[k, 2:8, :] = jnp.full((6, eb), nodes, jnp.int32)

    def copies(k):
        data = pltpu.make_async_remote_copy(
            src_ref=send.at[k],
            dst_ref=recv.at[k],
            send_sem=send_sem.at[k],
            recv_sem=recv_sem.at[k],
            device_id=at(me + k),
            device_id_type=MESH,
        )
        meta = pltpu.make_async_remote_copy(
            src_ref=meta_s.at[k],
            dst_ref=meta_r.at[k],
            send_sem=msend_sem.at[k],
            recv_sem=mrecv_sem.at[k],
            device_id=at(me + k),
            device_id_type=MESH,
        )
        return data, meta

    def send_step(i, carry):
        k = offset(i)
        fill(k)
        copies(k)[1].start()
        return carry

    def data_step(i, carry):
        copies(offset(i))[0].start()
        return carry

    lax.fori_loop(0, peers - 1, send_step, 0)
    lax.fori_loop(0, peers - 1, data_step, 0)
    fill(0)

    for n in late:
        loads[n].wait()
    mesh_bf = mesh_ref[...].astype(BF)
    ptab[...] = dot(mesh_bf, eei[ch:, :]).astype(BF)
    acc[...] = jnp.zeros_like(acc)
    cells = 68
    rows = nodes // 64
    s = msend_ref[...]
    a = lax.shift_right_logical(s * 241, 14)
    b_ = s - a * cells - W
    a = a - W
    above = a < 0
    below = a >= rows
    row_id = jnp.where(above, a + rows + W, jnp.where(below, a + W, a))
    local = jnp.where(above, a + rows, jnp.where(below, a - rows, a))
    which = jnp.where(above, 0, jnp.where(below, 2, 1))
    edge = W * 64
    halo = 2 * nodes
    base = halo + 2 * edge
    left = b_ < 0
    inner = (~left) & (b_ < 64)
    side = jnp.where(left, 0, 3)
    bb = jnp.where(left, b_ + W, b_ - 64)
    inside_id = row_id * 64 + b_ + jnp.where(row_id < rows, 0, nodes)
    cell = jnp.where(inner, inside_id, base + (side + which) * 16 + local * W + bb)
    cell_t = cell.astype(F32).T.astype(jnp.int32)
    mrecv = mrecv_ref[...]
    recv_base = nodes
    mrecv_t = (mrecv + recv_base).astype(F32).T.astype(jnp.int32)
    width = table.shape[0]
    lane_t = lax.broadcasted_iota(jnp.int32, (eb, width), 1)
    sub_n = lax.broadcasted_iota(jnp.int32, (nodes, eb), 0)
    for b in range(pblocks):
        hit = (cell_t[:, b : b + 1] == lane_t) | (mrecv_t[:, b : b + 1] == lane_t)
        oh[pl.ds(b * eb, eb), :] = one_hot(hit)
        oht[:, pl.ds(b * eb, eb)] = one_hot(sub_n == mrecv[b : b + 1, :])
        feat_t = mfeat_ref[b].astype(F32).T
        fbase[pl.ds(b * eb, eb), :] = feature_term(feat_t, pef) + peb[...]

    lane_n = lax.broadcasted_iota(jnp.int32, (eb, nodes), 1)

    def prepare(k, meta):
        ids = meta[...]
        ids_t = ids.astype(F32).T.astype(jnp.int32)
        for j in range(CAP):
            part = pl.ds(j * eb, eb)
            picks[k, part, :] = dot(one_hot(ids_t[:, j : j + 1] == lane_n), ptab[...])
            spread[k, :, part] = one_hot(sub_n == ids[j : j + 1, :])

    def encode(k, data):
        pre = picks[k] + data[...].astype(F32)
        hidden = silu(pre).astype(BF)
        edges = layer_norm(dot(hidden, eeo[...]), eeg[...]).astype(BF)
        acc[...] += dot(spread[k], edges)

    prepare(0, meta_s.at[0])
    encode(0, send.at[0])

    def meta_step(i, carry):
        k = offset(i)
        copies(k)[1].wait()
        prepare(k, meta_r.at[k])
        return carry

    lax.fori_loop(0, peers - 1, meta_step, 0)

    def recv_step(i, carry):
        k = offset(i)
        copies(k)[0].wait()
        encode(k, recv.at[k])
        return carry

    lax.fori_loop(0, peers - 1, recv_step, 0)

    def node(own_bf, summed, w_in, bias, w_out, gain):
        pre = dot(own_bf, w_in[:ch, :]) + dot(summed.astype(BF), w_in[ch:, :]) + bias[...]
        return layer_norm(dot(silu(pre).astype(BF), w_out[...]), gain[...])

    mesh_enc = mesh_ref[...] + node(mesh_bf, acc[...], eni, enb, eno, eng)
    menc[...] = mesh_enc
    enc_bf = mesh_enc.astype(BF)
    own = dot(enc_bf, pei[:ch, :]).astype(BF)
    table[0:nodes, :] = own
    pick_r = lax.broadcasted_iota(jnp.int32, (32, nodes), 0)
    pick_n = lax.broadcasted_iota(jnp.int32, (32, nodes), 1)
    r16 = pick_r & 15
    wanted = (r16 >> 1) * 64 + (r16 & 1) + jnp.where(pick_r < 16, 62, 0)
    packed = dot(one_hot(wanted == pick_n), own).astype(BF)
    packs[0] = packed[0:16]
    packs[1] = packed[16:32]

    def side_copy(dp, dl):
        n = (0 if dp == 1 else 3) + (1 - dl)
        return pltpu.make_async_remote_copy(
            src_ref=packs.at[0 if dp == 1 else 1],
            dst_ref=halo_packs.at[n],
            send_sem=hsend_sem.at[n],
            recv_sem=hrecv_sem.at[n],
            device_id=at(me + dp, lat + dl),
            device_id_type=MESH,
        )

    def band_copy(dl):
        n = 0 if dl == 1 else 1
        first = nodes - edge if dl == 1 else 0
        return pltpu.make_async_remote_copy(
            src_ref=table.at[pl.ds(first, edge), :],
            dst_ref=halo_rows.at[n],
            send_sem=hsend_sem.at[6 + n],
            recv_sem=hrecv_sem.at[6 + n],
            device_id=at(me, lat + dl),
            device_id_type=MESH,
        )

    def inside(dl):
        return (lat + dl >= 0) & (lat + dl < lats)

    for dl in (-1, 1):

        @pl.when(inside(dl))
        def _():
            band_copy(dl).start()
            side_copy(1, dl).start()
            side_copy(-1, dl).start()

    side_copy(1, 0).start()
    side_copy(-1, 0).start()
    table[recv_base : recv_base + nodes, :] = dot(enc_bf, pei[ch:, :]).astype(BF)
    table[base + 96 :, :] = jnp.zeros((width - base - 96, ch), BF)
    step = 4 * eb
    chunks = pblocks * eb // step
    for i in range(chunks):
        part = pl.ds(i * step, step)
        fbase[part, :] += dot(oh[part, :halo], table[:halo, :])
    own_in = dot(enc_bf, pni[:ch, :]) + pnb[...]

    for dl in (-1, 1):
        n = 0 if dl == -1 else 1
        slots = (0, 3) if dl == -1 else (2, 5)

        @pl.when(inside(dl))
        def _():
            band_copy(-dl).wait_recv()
            side_copy(1, -dl).wait_recv()
            side_copy(-1, -dl).wait_recv()
            table[pl.ds(halo + n * edge, edge), :] = halo_rows[n]
            for m in slots:
                table[pl.ds(base + m * 16, 16), :] = halo_packs[m]

        @pl.when(jnp.logical_not(inside(dl)))
        def _():
            table[pl.ds(halo + n * edge, edge), :] = jnp.zeros((edge, ch), BF)
            for m in slots:
                table[pl.ds(base + m * 16, 16), :] = jnp.zeros((16, ch), BF)

    side_copy(1, 0).wait_recv()
    side_copy(-1, 0).wait_recv()
    table[pl.ds(base + 16, 16), :] = halo_packs[1]
    table[pl.ds(base + 64, 16), :] = halo_packs[4]

    for i in range(chunks):
        part = pl.ds(i * step, step)
        pre = fbase[part, :] + dot(oh[part, halo:], table[halo:, :])
        projected = dot(silu(pre).astype(BF), peo[...])
        pedges[part, :] = layer_norm(projected, peg[...]).astype(BF)
    summed = dot(oht[...], pedges[...])
    pre = own_in + dot(summed.astype(BF), pni[ch:, :])
    out_ref[...] = menc[...] + layer_norm(dot(silu(pre).astype(BF), pno[...]), png[...])

    for dl in (-1, 1):

        @pl.when(inside(dl))
        def _():
            band_copy(dl).wait_send()
            side_copy(1, dl).wait_send()
            side_copy(-1, dl).wait_send()

    side_copy(1, 0).wait_send()
    side_copy(-1, 0).wait_send()


def on_device(
    grid_latent,
    mesh_latent,
    block_owner,
    block_sender,
    block_receiver,
    block_feature,
    mesh_sender,
    mesh_receiver,
    mesh_feature,
    *weights,
):
    subs = lax.axis_size("sub")
    peers = lax.axis_size("lon") * subs
    lats = lax.axis_size("lat")
    rows_lat, rows_lon, ch = mesh_latent.shape
    nodes = rows_lat * rows_lon
    blocks, eb = block_sender.shape
    pblocks = mesh_sender.shape[0]
    weights = [w.reshape(1, -1) if w.ndim == 1 else w for w in weights]
    width = 1408
    inputs = [
        grid_latent,
        mesh_latent.reshape(nodes, ch),
        block_owner.reshape(1, blocks),
        block_sender,
        block_receiver,
        block_feature,
        mesh_sender,
        mesh_receiver,
        mesh_feature,
        *weights,
    ]
    staged = [
        (pltpu.SMEM if n == 2 else pltpu.VMEM)(x.shape, x.dtype) for n, x in enumerate(inputs)
    ]
    dma = pltpu.SemaphoreType.DMA
    out = pl.pallas_call(
        functools.partial(kernel, peers, subs, lats),
        out_shape=jax.ShapeDtypeStruct((nodes, ch), F32),
        in_specs=[pl.BlockSpec(memory_space=pl.ANY)] * len(inputs),
        out_specs=pl.BlockSpec(memory_space=pltpu.VMEM),
        scratch_shapes=[
            pltpu.VMEM(grid_latent.shape, BF),
            pltpu.VMEM((blocks, eb, ch), BF),
            pltpu.VMEM((peers, CAP * eb, ch), BF),
            pltpu.VMEM((peers, 8, eb), jnp.int32),
            pltpu.VMEM((peers, CAP * eb, ch), BF),
            pltpu.VMEM((peers, 8, eb), jnp.int32),
            pltpu.VMEM((nodes, ch), F32),
            pltpu.VMEM((nodes, ch), BF),
            pltpu.VMEM((width, ch), BF),
            pltpu.VMEM((2, 16, ch), BF),
            pltpu.VMEM((2, W * rows_lon, ch), BF),
            pltpu.VMEM((6, 16, ch), BF),
            pltpu.VMEM((nodes, ch), F32),
            pltpu.VMEM((pblocks * eb, width), BF),
            pltpu.VMEM((nodes, pblocks * eb), BF),
            pltpu.VMEM((pblocks * eb, ch), F32),
            pltpu.VMEM((pblocks * eb, ch), BF),
            pltpu.VMEM((peers, CAP * eb, ch), F32),
            pltpu.VMEM((peers, nodes, CAP * eb), BF),
            dma((peers,)),
            dma((peers,)),
            dma((peers,)),
            dma((peers,)),
            dma((8,)),
            dma((8,)),
            dma((len(inputs),)),
        ]
        + staged,
        compiler_params=pltpu.CompilerParams(
            collective_id=0, has_side_effects=True, vmem_limit_bytes=64 * 1024 * 1024
        ),
    )(*inputs)
    return out.reshape(rows_lat, rows_lon, ch)


def solution(mesh):
    band = P(("lon", "lat", "sub"), None)
    band3 = P(("lon", "lat", "sub"), None, None)
    place = P(("groups", "lat"), ("lon", "sub"), None)
    in_specs = (
        P(("groups", "lon", "lat", "sub"), None),
        place,
        band,
        band,
        band,
        band3,
        band,
        band,
        band3,
    ) + (P(),) * 18
    return jax.shard_map(
        on_device, mesh=mesh, in_specs=in_specs, out_specs=place, check_vma=False
    )
```
